32 devices in a mesh: dp: 8 (over y, x, core), ctx: 4 (over z).
Axes of the slice: x: 2, y: 2, z: 4, core: 2. Of those that a mesh axis runs over, the one named last changes fastest.
Arguments:
- tokens: bfloat16 [8192, 960], P(('dp', 'ctx')), may hold values from -6 to 6
- w_query: bfloat16 [921600], P(('dp', 'ctx')), may hold values from -0.1875 to 0.1875
- w_key: bfloat16 [307200], P(('dp', 'ctx')), may hold values from -0.1875 to 0.1875
- w_value: bfloat16 [307200], P(('dp', 'ctx')), may hold values from -0.1875 to 0.1875
- w_out: bfloat16 [921600], P(('dp', 'ctx')), may hold values from -6 to 6
- w_gate: bfloat16 [2457600], P(('dp', 'ctx')), may hold values from -0.1875 to 0.1875
- w_up: bfloat16 [2457600], P(('dp', 'ctx')), may hold values from -0.1875 to 0.1875
- w_down: bfloat16 [2457600], P(('dp', 'ctx')), may hold values from -0.125 to 0.125
- norm_gains: bfloat16 [2, 960], P(None, 'dp'), may hold values from 0.5 to 1.5
- cotangent: bfloat16 [8192, 960], P(('dp', 'ctx')), may hold values from -6 to 6
Outputs:
- layer_out: bfloat16 [8192, 960], P(('dp', 'ctx'))
- grad_tokens: bfloat16 [8192, 960], P(('dp', 'ctx'))
- grad_query: float32 [921600], P(('dp', 'ctx'))
- grad_key: float32 [307200], P(('dp', 'ctx'))
- grad_value: float32 [307200], P(('dp', 'ctx'))
- grad_out: float32 [921600], P(('dp', 'ctx'))
- grad_gate: float32 [2457600], P(('dp', 'ctx'))
- grad_up: float32 [2457600], P(('dp', 'ctx'))
- grad_down: float32 [2457600], P(('dp', 'ctx'))
- grad_gains: float32 [2, 960], P(None, 'dp')
The draws below stay inside these ranges and needn't reach their ends.
All inputs are finite; a program needn't handle non-finite values.
Results may differ from the reference program's by a relative error of at most 0.019.
Values may be sent and summed in bfloat16 or wider, within the bound.
A program may use at most 192 MiB of HBM per device.

```python
import math
import jax
import jax.numpy as jnp
from jax import lax

D = 960
FF = 2560
HEADS = 15
KV_HEADS = 5
HEAD_DIM = 64
TOK_DEV = 256
TOKENS = 8192
N_DP = 8
N_CTX = 4


def shard_levels(own_key, dims, split, least, top_value):
    level, own = 1.0, jax.random.fold_in(own_key, 6)
    for dim, shards_of in split:
        steps = jnp.exp(jax.random.uniform(jax.random.fold_in(own, dim), (shards_of,), jnp.float32, least / len(split), top_value / len(split)))
        level = level * jnp.repeat(steps, dims[dim] // shards_of).reshape([-1 if axis == dim else 1 for axis in range(len(dims))])
    return level


def scatter_about(own_key, shape, width, limit, split=(), kind=jnp.bfloat16):
    factor_of = shard_levels(own_key, shape, split, -0.22, 0.18) if split else 1.0
    drawn = jax.random.normal(own_key, shape, jnp.float32) * width * factor_of
    return jnp.minimum(jnp.maximum(drawn, -limit), limit).astype(kind)


def setup_inputs(seed: int = 0) -> dict:
    key_of = jax.random.split(jax.random.key(seed), 11)
    tokens = scatter_about(key_of[0], (TOKENS, D), 1.0, 6.0, ((0, 32),))
    w_query = scatter_about(key_of[1], (D * HEADS * HEAD_DIM,), D ** -0.5, 0.1875, ((0, 32),))
    w_key = scatter_about(key_of[2], (D * KV_HEADS * HEAD_DIM,), D ** -0.5, 0.1875, ((0, 32),))
    w_value = scatter_about(key_of[3], (D * KV_HEADS * HEAD_DIM,), D ** -0.5, 0.1875, ((0, 32),))
    w_out = scatter_about(key_of[4], (HEADS * HEAD_DIM * D,), (max(1, 2 * HEADS * HEAD_DIM // (TOK_DEV * N_CTX))) ** -0.5, 6.0, ((0, 32),))
    w_gate = scatter_about(key_of[5], (D * FF,), D ** -0.5, 0.1875, ((0, 32),))
    w_up = scatter_about(key_of[6], (D * FF,), D ** -0.5, 0.1875, ((0, 32),))
    w_down = scatter_about(key_of[7], (FF * D,), FF ** -0.5, 0.125, ((0, 32),))
    norm_gains = jnp.clip(1.0 + 0.1 * jax.random.normal(key_of[8], (2, D), jnp.float32), 0.5, 1.5).astype(jnp.bfloat16)
    cotangent = scatter_about(key_of[9], (TOKENS, D), 1.0, 6.0, ((0, 32),))
    return dict(tokens=tokens, w_query=w_query, w_key=w_key, w_value=w_value, w_out=w_out, w_gate=w_gate, w_up=w_up, w_down=w_down, norm_gains=norm_gains, cotangent=cotangent)


@jax.custom_vjp
def low(v):
    return lax.optimization_barrier(v.astype(jnp.bfloat16)).astype(jnp.float32)

@jax.custom_vjp
def low_back(v):
    return v

def low_keep(v):
    return (low(v), None)

def low_pass(kept, grad):
    return (grad,)

def back_keep(v):
    return (v, None)

def back_low(kept, grad):
    return (low(grad),)
low.defvjp(low_keep, low_pass)
low_back.defvjp(back_keep, back_low)
EPSILON = 1e-05
THETA = 100000.0

def product(left, right):
    return jnp.dot(left, right, precision=lax.Precision.HIGHEST, preferred_element_type=jnp.float32)

def rms_scale(values, gain):
    return values * lax.rsqrt(lax.optimization_barrier(jnp.mean(values * values, axis=-1, keepdims=True)) + EPSILON) * gain

def rotate(values, places):
    half = HEAD_DIM // 2
    frequency = THETA ** (-jnp.arange(half, dtype=jnp.float32) * 2.0 / HEAD_DIM)
    angle = places.astype(jnp.float32)[:, None] * frequency[None, :]
    cosine = jnp.cos(angle)[:, None, :]
    sine = jnp.sin(angle)[:, None, :]
    shaped = values.reshape(values.shape[0], -1, HEAD_DIM)
    first = shaped[..., :half]
    second = shaped[..., half:]
    turned = jnp.concatenate([first * cosine - second * sine, second * cosine + first * sine], axis=-1)
    return turned.reshape(values.shape)

def layer(inputs, w_query, w_key, w_value, w_out, w_gate, w_up, w_down, gains):
    length = inputs.shape[0]
    groups = HEADS // KV_HEADS
    places = jnp.arange(length, dtype=jnp.int32)
    normed = low(rms_scale(inputs, gains[0]))
    query = low(rotate(low_back(product(normed, w_query)), places))
    key = low(rotate(low_back(product(normed, w_key)), places))
    value = low(low_back(product(normed, w_value)))
    query_heads = query.reshape(length, KV_HEADS, groups, HEAD_DIM)
    key_heads = key.reshape(length, KV_HEADS, HEAD_DIM)
    value_heads = value.reshape(length, KV_HEADS, HEAD_DIM)
    block = math.gcd(length, 512)

    def attend(item):
        query_block, start = item
        query_places = start + jnp.arange(block, dtype=jnp.int32)
        scores = jnp.einsum('qgrd,kgd->grqk', query_block, key_heads, precision=lax.Precision.HIGHEST) * HEAD_DIM ** (-0.5)
        scores = low_back(scores)
        allowed = query_places[:, None] >= places[None, :]
        scores = jnp.where(allowed, scores, -1e+30)
        weights = low(jax.nn.softmax(scores, axis=-1))
        return jnp.einsum('grqk,kgd->qgrd', weights, value_heads, precision=lax.Precision.HIGHEST)
    query_blocks = query_heads.reshape(length // block, block, KV_HEADS, groups, HEAD_DIM)
    starts = jnp.arange(length // block, dtype=jnp.int32) * block
    mixed = lax.map(jax.checkpoint(attend), (query_blocks, starts))
    mixed = low(low_back(mixed.reshape(length, HEADS * HEAD_DIM)))
    hidden = inputs + low_back(product(mixed, w_out))
    normed_two = low(rms_scale(hidden, gains[1]))
    gate_values = low_back(product(normed_two, w_gate))
    up_values = low_back(product(normed_two, w_up))
    active = low(jax.nn.silu(gate_values) * up_values)
    return hidden + low_back(product(active, w_down))

def reference(tokens, w_query, w_key, w_value, w_out, w_gate, w_up, w_down, norm_gains, cotangent):
    query_width = HEADS * HEAD_DIM
    pair_width = KV_HEADS * HEAD_DIM
    matrices = (w_query.astype(jnp.float32).reshape(D, query_width), w_key.astype(jnp.float32).reshape(D, pair_width), w_value.astype(jnp.float32).reshape(D, pair_width), w_out.astype(jnp.float32).reshape(query_width, D), w_gate.astype(jnp.float32).reshape(D, FF), w_up.astype(jnp.float32).reshape(D, FF), w_down.astype(jnp.float32).reshape(FF, D))
    gains = norm_gains.astype(jnp.float32)
    length = TOK_DEV * N_CTX
    sequences = tokens.astype(jnp.float32).reshape(N_DP, length, D)
    cotangents = cotangent.astype(jnp.float32).reshape(N_DP, length, D)

    def step(totals, item):
        inputs, seed_grad = item
        result, pull = jax.vjp(layer, inputs, *matrices, gains)
        grads = pull(seed_grad)
        totals = tuple((total + grad for total, grad in zip(totals, grads[1:])))
        return (totals, (result, grads[0]))
    start = tuple((jnp.zeros(matrix.shape, jnp.float32) for matrix in matrices)) + (jnp.zeros(gains.shape, jnp.float32),)
    totals, (results, input_grads) = lax.scan(step, start, (sequences, cotangents))
    layer_out = results.reshape(N_DP * length, D).astype(jnp.bfloat16)
    grad_tokens = input_grads.reshape(N_DP * length, D).astype(jnp.bfloat16)
    return (layer_out, grad_tokens, totals[0].reshape(-1), totals[1].reshape(-1), totals[2].reshape(-1), totals[3].reshape(-1), totals[4].reshape(-1), totals[5].reshape(-1), totals[6].reshape(-1), totals[7])
```

```python
import functools

import jax
import jax.numpy as jnp
from jax import lax
from jax.sharding import PartitionSpec as P

D = 960
FF = 2560
HEADS = 15
KV_HEADS = 5
HEAD_DIM = 64


EPSILON = 1e-05
THETA = 100000.0


def product(left, right):
    return jnp.dot(left, right, preferred_element_type=jnp.float32)


def product_left(left, right):
    return lax.dot_general(
        left, right, (((0,), (0,)), ((), ())), preferred_element_type=jnp.float32
    )


def product_right(left, right):
    return lax.dot_general(
        left, right, (((1,), (1,)), ((), ())), preferred_element_type=jnp.float32
    )


LOW = jnp.bfloat16
BOTH = ("dp", "ctx")


def swap(values, axis, size, mask):
    return lax.ppermute(values, axis, [(index, index ^ mask) for index in range(size)])


def bits_of(size):
    return [1 << place for place in range(size.bit_length() - 1)]


class Exchange:
    def __init__(self, dp_size, ctx_size, dp_bits):
        stages = [("ctx", mask) for mask in reversed(bits_of(ctx_size))]
        stages += [("dp", mask) for mask in dp_bits] + [("dp", 1)]
        self.stages = stages
        self.sizes = {"dp": dp_size, "ctx": ctx_size}
        self.count = dp_size * ctx_size
        slots = jnp.arange(self.count, dtype=jnp.int32)
        place = {"dp": lax.axis_index("dp"), "ctx": lax.axis_index("ctx")}
        for index, (axis, mask) in enumerate(stages):
            place[axis] = place[axis] ^ (((slots >> index) & 1) * mask)
        self.shard = place["dp"] * ctx_size + place["ctx"]

    def gather(self, block):
        for axis, mask in self.stages:
            block = jnp.concatenate([block, swap(block, axis, self.sizes[axis], mask)], axis=0)
        return block

    def scatter(self, keep, send):
        for index, (axis, mask) in enumerate(reversed(self.stages)):
            got = swap(send.astype(LOW), axis, self.sizes[axis], mask)
            total = keep.astype(jnp.float32) + got.astype(jnp.float32)
            half = total.shape[0] // 2
            if index < len(self.stages) - 1:
                total = total.astype(LOW)
                keep, send = total[:half], total[half:]
        return total

    def selection(self, rows, padded):
        column = jnp.arange(padded, dtype=jnp.int32)
        source = jnp.where(column < rows, self.shard[:, None] * rows + column, -1).reshape(-1)
        feature = jnp.arange(self.count * rows, dtype=jnp.int32)
        return (feature[:, None] == source[None, :]).astype(LOW)


class RowWeights:
    def __init__(self, exchange, rows):
        self.exchange, self.rows = exchange, rows
        self.padded = -(-rows // 16) * 16
        self.select = exchange.selection(rows, self.padded)

    def gather(self, flats, widths):
        block = jnp.concatenate(
            [flat.reshape(self.rows, width) for flat, width in zip(flats, widths)], axis=1
        )
        return self.exchange.gather(jnp.pad(block, ((0, self.padded - self.rows), (0, 0))))

    def spread(self, values):
        return product(values, self.select).astype(LOW)

    def unspread(self, values):
        upper = values.astype(LOW)
        lower = (values - upper.astype(jnp.float32)).astype(LOW)
        return product_right(upper, self.select) + product_right(lower, self.select)

    def scatter(self, left, right, widths):
        half = left.shape[1] // 2
        send = product_left(left[:, half:], right).astype(LOW)
        total = self.exchange.scatter(product_left(left[:, :half], right), send)[: self.rows]
        cuts = [sum(widths[:index]) for index in range(len(widths) + 1)]
        return [total[:, low:high].reshape(-1) for low, high in zip(cuts[:-1], cuts[1:])]


class FlatWeights:
    def gather(self, flats, widths):
        return jnp.concatenate(
            [
                lax.all_gather(flat, BOTH, axis=0, tiled=True).reshape(-1, width)
                for flat, width in zip(flats, widths)
            ],
            axis=1,
        )

    def spread(self, values):
        return values.astype(LOW)

    def unspread(self, values):
        return values

    def scatter(self, left, right, widths):
        cuts = [sum(widths[:index]) for index in range(len(widths) + 1)]
        return [
            lax.psum_scatter(
                product_left(left, right[:, low:high]).astype(LOW).reshape(-1),
                BOTH,
                scatter_dimension=0,
                tiled=True,
            ).astype(jnp.float32)
            for low, high in zip(cuts[:-1], cuts[1:])
        ]


def rope_tables(places):
    half = HEAD_DIM // 2
    frequency = THETA ** (-jnp.arange(half, dtype=jnp.float32) * 2.0 / HEAD_DIM)
    angle = places.astype(jnp.float32)[:, None] * frequency[None, :]
    return (jnp.cos(angle)[:, None, :], jnp.sin(angle)[:, None, :])


def rotate(values, cosine, sine, direction):
    half = HEAD_DIM // 2
    shaped = values.reshape(values.shape[0], -1, HEAD_DIM)
    first = shaped[..., :half]
    second = shaped[..., half:]
    turned = jnp.concatenate(
        [first * cosine - direction * second * sine, second * cosine + direction * first * sine],
        axis=-1,
    )
    return turned.reshape(values.shape)


def rms_forward(values, gain):
    factor = lax.rsqrt(jnp.mean(values * values, axis=-1, keepdims=True) + EPSILON)
    return (values * factor * gain, factor)


def rms_backward(values, factor, gain, grad):
    inner = grad * gain
    gain_grad = jnp.sum(grad * values * factor, axis=0)
    cube = factor * factor * factor
    input_grad = factor * inner - values * cube * jnp.mean(inner * values, axis=-1, keepdims=True)
    return (input_grad, gain_grad)


def per_device(
    dp_size,
    ctx_size,
    tokens,
    w_query,
    w_key,
    w_value,
    w_out,
    w_gate,
    w_up,
    w_down,
    norm_gains,
    cotangent,
):
    local_rows = tokens.shape[0]
    query_width = HEADS * HEAD_DIM
    pair_width = KV_HEADS * HEAD_DIM
    groups = HEADS // KV_HEADS
    scale = HEAD_DIM ** (-0.5)
    devices = dp_size * ctx_size
    by_rows = D % devices == 0 and FF % devices == 0

    qkv_widths = (query_width, pair_width, pair_width)
    if by_rows:
        dp_bits = bits_of(dp_size)[1:]
        exchange_up = Exchange(dp_size, ctx_size, dp_bits)
        exchange_down = Exchange(dp_size, ctx_size, dp_bits[::-1])
        attn = RowWeights(exchange_up, D // devices)
        feed = RowWeights(exchange_down, D // devices)
        last_rows = FF // devices
    else:
        attn = feed = FlatWeights()

    gains = lax.all_gather(norm_gains, "dp", axis=1, tiled=True).astype(jnp.float32)
    qkv_matrix = attn.gather((w_query, w_key, w_value), qkv_widths)
    out_matrix = attn.gather((w_out,), (D,))
    feed_matrix = feed.gather((w_gate, w_up), (FF, FF))
    if by_rows:
        slots = exchange_up.gather(w_down.reshape(1, last_rows, D))
        down_matrix = jnp.take(slots, jnp.argsort(exchange_up.shard), axis=0).reshape(FF, D)
    else:
        down_matrix = feed.gather((w_down,), (D,))

    ctx_place = lax.axis_index("ctx")
    inner = jnp.arange(local_rows, dtype=jnp.int32)
    places = ctx_place * local_rows + inner
    others = ctx_place ^ jnp.arange(ctx_size, dtype=jnp.int32)
    key_places = (others[:, None] * local_rows + inner[None, :]).reshape(-1)
    cosine, sine = rope_tables(places)

    inputs = tokens.astype(jnp.float32)
    scaled_first, rms_first = rms_forward(inputs, gains[0])
    normed_first = attn.spread(scaled_first.astype(LOW))
    projected = product(normed_first, qkv_matrix)
    query = rotate(projected[:, :query_width], cosine, sine, 1.0).astype(LOW)
    key = rotate(projected[:, query_width : query_width + pair_width], cosine, sine, 1.0)
    pairs = jnp.concatenate([key.astype(LOW), projected[:, query_width + pair_width :].astype(LOW)], 1)
    whole = jnp.concatenate(
        [pairs] + [swap(pairs, "ctx", ctx_size, mask) for mask in range(1, ctx_size)], axis=0
    )
    count = whole.shape[0]

    def by_head(values):
        shaped = values.reshape(local_rows, KV_HEADS, groups, HEAD_DIM).transpose(1, 2, 0, 3)
        return shaped.reshape(KV_HEADS, groups * local_rows, HEAD_DIM)

    def by_token(values):
        shaped = values.reshape(KV_HEADS, groups, local_rows, HEAD_DIM).transpose(2, 0, 1, 3)
        return shaped.reshape(local_rows, query_width)

    def batched(pattern, left, right):
        return jnp.einsum(pattern, left, right, preferred_element_type=jnp.float32)

    query_heads = by_head(query)
    key_heads = whole[:, :pair_width].reshape(count, KV_HEADS, HEAD_DIM).transpose(1, 0, 2)
    value_heads = whole[:, pair_width:].reshape(count, KV_HEADS, HEAD_DIM).transpose(1, 0, 2)
    allowed = jnp.tile(places, groups)[:, None] >= key_places[None, :]
    scores = batched("gqd,gkd->gqk", query_heads, key_heads) * scale
    scores = jnp.where(allowed[None], scores, -1e30)
    top = jnp.max(scores, axis=-1, keepdims=True)
    unscaled = jnp.exp(scores - top)
    weights = unscaled * (1.0 / jnp.sum(unscaled, axis=-1, keepdims=True))
    weights_low = weights.astype(LOW)
    mixed_heads = batched("gqk,gkd->gqd", weights_low, value_heads)
    mixed_low = attn.spread(by_token(mixed_heads.astype(LOW)))

    hidden = inputs + product(mixed_low, out_matrix)
    scaled_second, rms_second = rms_forward(hidden, gains[1])
    normed_second = feed.spread(scaled_second.astype(LOW))
    gate_up = product(normed_second, feed_matrix)
    gate_values, up_values = gate_up[:, :FF], gate_up[:, FF:]
    sigmoid_gate = jax.nn.sigmoid(gate_values)
    silu_gate = gate_values * sigmoid_gate
    active = (silu_gate * up_values).astype(LOW)
    layer_out = (hidden + product(active, down_matrix)).astype(LOW)

    if by_rows:
        blocks = product_left(active, cotangent).astype(LOW).reshape(devices, last_rows, D)
        blocks = jnp.take(blocks, exchange_up.shard, axis=0)
        grad_down = exchange_up.scatter(blocks[: devices // 2], blocks[devices // 2 :]).reshape(-1)
    else:
        (grad_down,) = feed.scatter(active, cotangent, (D,))
    grad_layer = cotangent.astype(jnp.float32)
    grad_active = product_right(cotangent, down_matrix)
    grad_gate_values = grad_active * up_values * (
        sigmoid_gate * (1.0 + gate_values * (1.0 - sigmoid_gate))
    )
    grad_feed = jnp.concatenate(
        [grad_gate_values.astype(LOW), (grad_active * silu_gate).astype(LOW)], axis=1
    )
    grad_gate, grad_up = feed.scatter(normed_second, grad_feed, (FF, FF))
    grad_normed_second = feed.unspread(product_right(grad_feed, feed_matrix))
    grad_hidden_norm, gain_second = rms_backward(hidden, rms_second, gains[1], grad_normed_second)
    grad_hidden = grad_layer + grad_hidden_norm
    grad_attn = grad_hidden.astype(LOW)
    (grad_out,) = attn.scatter(mixed_low, grad_attn, (D,))
    grad_mixed = attn.unspread(product_right(grad_attn, out_matrix)).astype(LOW)

    grad_heads = by_head(grad_mixed)
    delta = jnp.sum(grad_heads.astype(jnp.float32) * mixed_heads, axis=-1, keepdims=True)
    grad_weights = batched("gqd,gkd->gqk", grad_heads, value_heads)
    grad_scores = (weights * (grad_weights - delta)).astype(LOW)
    grad_key_all = batched("gqk,gqd->gkd", grad_scores, query_heads) * scale
    grad_value_all = batched("gqk,gqd->gkd", weights_low, grad_heads)
    grad_query_heads = batched("gqk,gkd->gqd", grad_scores, key_heads) * scale
    term = jnp.concatenate([grad_key_all, grad_value_all], axis=0)
    term = term.transpose(1, 0, 2).reshape(ctx_size, local_rows, 2 * pair_width)
    pair_grads = term[0]
    for mask in range(1, ctx_size):
        pair_grads += swap(term[mask].astype(LOW), "ctx", ctx_size, mask).astype(jnp.float32)
    grad_projected = jnp.concatenate(
        [
            rotate(by_token(grad_query_heads), cosine, sine, -1.0).astype(LOW),
            rotate(pair_grads[:, :pair_width], cosine, sine, -1.0).astype(LOW),
            pair_grads[:, pair_width:].astype(LOW),
        ],
        axis=1,
    )
    grad_query, grad_key, grad_value = attn.scatter(normed_first, grad_projected, qkv_widths)
    grad_normed_first = attn.unspread(product_right(grad_projected, qkv_matrix))
    grad_input_norm, gain_first = rms_backward(inputs, rms_first, gains[0], grad_normed_first)
    grad_tokens = (grad_hidden + grad_input_norm).astype(LOW)
    gain_all = lax.psum(jnp.stack([gain_first, gain_second]), BOTH)
    gain_width = norm_gains.shape[1]
    gain_total = lax.dynamic_slice_in_dim(gain_all, lax.axis_index("dp") * gain_width, gain_width, 1)
    return (
        layer_out,
        grad_tokens,
        grad_query,
        grad_key,
        grad_value,
        grad_out,
        grad_gate,
        grad_up,
        grad_down,
        gain_total,
    )


def solution(mesh):
    placed = (
        P(("dp", "ctx"), None),
        P(("dp", "ctx")),
        P(("dp", "ctx")),
        P(("dp", "ctx")),
        P(("dp", "ctx")),
        P(("dp", "ctx")),
        P(("dp", "ctx")),
        P(("dp", "ctx")),
        P(None, "dp"),
        P(("dp", "ctx"), None),
    )
    dp_size, ctx_size = mesh.shape["dp"], mesh.shape["ctx"]
    return jax.shard_map(
        functools.partial(per_device, dp_size, ctx_size),
        mesh=mesh,
        in_specs=placed,
        out_specs=(
            P(("dp", "ctx"), None),
            P(("dp", "ctx"), None),
            P(("dp", "ctx")),
            P(("dp", "ctx")),
            P(("dp", "ctx")),
            P(("dp", "ctx")),
            P(("dp", "ctx")),
            P(("dp", "ctx")),
            P(("dp", "ctx")),
            P(None, "dp"),
        ),
        check_vma=False,
    )
```

```python
import functools

import jax
import jax.numpy as jnp
from jax import lax
from jax.sharding import PartitionSpec as P

D = 960
FF = 2560
HEADS = 15
KV_HEADS = 5
HEAD_DIM = 64


EPSILON = 1e-05
THETA = 100000.0


def product(left, right):
    return jnp.dot(left, right, preferred_element_type=jnp.float32)


def product_left(left, right):
    return lax.dot_general(
        left, right, (((0,), (0,)), ((), ())), preferred_element_type=jnp.float32
    )


def product_right(left, right):
    return lax.dot_general(
        left, right, (((1,), (1,)), ((), ())), preferred_element_type=jnp.float32
    )


LOW = jnp.bfloat16
BOTH = ("dp", "ctx")


def swap(values, axis, size, mask):
    return lax.ppermute(values, axis, [(index, index ^ mask) for index in range(size)])


def bits_of(size):
    return [1 << place for place in range(size.bit_length() - 1)]


class Exchange:
    def __init__(self, dp_size, ctx_size, stages):
        self.stages = stages
        self.sizes = {"dp": dp_size, "ctx": ctx_size}
        self.count = 1 << len(stages)
        slots = jnp.arange(self.count, dtype=jnp.int32)
        place = {"dp": lax.axis_index("dp"), "ctx": lax.axis_index("ctx")}
        for index, (axis, mask) in enumerate(stages):
            place[axis] = place[axis] ^ (((slots >> index) & 1) * mask)
        self.shard = place["dp"] * ctx_size + place["ctx"]

    def gather(self, block):
        for axis, mask in self.stages:
            block = jnp.concatenate([block, swap(block, axis, self.sizes[axis], mask)], axis=0)
        return block

    def scatter(self, keep, send):
        for index, (axis, mask) in enumerate(reversed(self.stages)):
            got = swap(send.astype(LOW), axis, self.sizes[axis], mask)
            total = keep.astype(jnp.float32) + got.astype(jnp.float32)
            half = total.shape[0] // 2
            if index < len(self.stages) - 1:
                total = total.astype(LOW)
                keep, send = total[:half], total[half:]
        return total

    def selection(self, rows, padded):
        column = jnp.arange(padded, dtype=jnp.int32)
        source = jnp.where(column < rows, self.shard[:, None] * rows + column, -1).reshape(-1)
        feature = jnp.arange(self.count * rows, dtype=jnp.int32)
        return (feature[:, None] == source[None, :]).astype(LOW)


def sum_gains(values, dp_size, ctx_size):
    width = values.shape[1] // dp_size
    slots = lax.axis_index("dp") ^ jnp.arange(dp_size, dtype=jnp.int32)
    blocks = jnp.take(values.reshape(2, dp_size, width).transpose(1, 0, 2), slots, axis=0)
    for mask in reversed(bits_of(dp_size)):
        blocks = blocks[:mask] + swap(blocks[mask:], "dp", dp_size, mask)
    for mask in bits_of(ctx_size):
        blocks = blocks + swap(blocks, "ctx", ctx_size, mask)
    return blocks[0]


class RowWeights:
    def __init__(self, exchange, rows):
        self.exchange, self.rows = exchange, rows
        self.padded = -(-rows // 16) * 16
        self.select = exchange.selection(rows, self.padded)

    def gather(self, flats, widths):
        block = jnp.concatenate(
            [flat.reshape(self.rows, width) for flat, width in zip(flats, widths)], axis=1
        )
        return self.exchange.gather(jnp.pad(block, ((0, self.padded - self.rows), (0, 0))))

    def spread(self, values):
        return product(values, self.select).astype(LOW)

    def unspread(self, values):
        upper = values.astype(LOW)
        lower = (values - upper.astype(jnp.float32)).astype(LOW)
        return product_right(upper, self.select) + product_right(lower, self.select)

    def scatter(self, left, right, widths):
        half = left.shape[1] // 2
        send = product_left(left[:, half:], right).astype(LOW)
        right, send = lax.optimization_barrier((right, send))
        total = self.exchange.scatter(product_left(left[:, :half], right), send)[: self.rows]
        cuts = [sum(widths[:index]) for index in range(len(widths) + 1)]
        return right, [total[:, low:high].reshape(-1) for low, high in zip(cuts[:-1], cuts[1:])]


class SplitFeed:
    def __init__(self, dp_size, ctx_size, rows, last_rows, up_bits, down_bits):
        near = [("ctx", mask) for mask in reversed(bits_of(ctx_size))]
        core = [("dp", 1)]
        self.outer = Exchange(dp_size, ctx_size, near + [("dp", mask) for mask in up_bits])
        self.down = Exchange(dp_size, ctx_size, near + [("dp", mask) for mask in down_bits])
        order = Exchange(dp_size, ctx_size, core + self.outer.stages)
        self.weights = RowWeights(order, rows)
        self.rows, self.last_rows, self.dp_size = rows, last_rows, dp_size
        self.core = lax.axis_index("dp") % 2
        self.run = ctx_size * last_rows
        self.ranks = self.down.shard // ctx_size // 2 * ctx_size + self.down.shard % ctx_size

    def partner(self, values):
        return swap(values, "dp", self.dp_size, 1)

    def gather(self, gate, up, down):
        block = jnp.stack([flat.reshape(self.rows, -1, 2, self.run) for flat in (gate, up)], axis=1)
        padding = ((0, self.weights.padded - self.rows), (0, 0))
        first, second = (
            jnp.pad(block[:, :, :, core].reshape(self.rows, -1), padding) for core in range(2)
        )
        keep = jnp.where(self.core == 0, first, second)
        send = jnp.where(self.core == 0, second, first)
        matrix = self.outer.gather(jnp.concatenate([keep, self.partner(send)], axis=0))
        slots = self.down.gather(down.reshape(1, self.last_rows, D))
        return matrix, jnp.take(slots, jnp.argsort(self.ranks), axis=0).reshape(-1, D)

    def both(self, values):
        return jnp.concatenate([values, self.partner(values)], axis=0)

    def own(self, values):
        half = values.shape[0] // 2
        return values[:half] + self.partner(values[half:].astype(LOW)).astype(jnp.float32)

    def scatter_down(self, active, cotangent):
        blocks = product_left(active, cotangent).astype(LOW).reshape(-1, self.last_rows, D)
        blocks = jnp.take(blocks, self.ranks, axis=0)
        cotangent, blocks = lax.optimization_barrier((cotangent, blocks))
        half = blocks.shape[0] // 2
        return cotangent, self.down.scatter(blocks[:half], blocks[half:]).reshape(-1)

    def scatter(self, left, right):
        half = left.shape[1] // 2
        send = product_left(left[:, half:], right).astype(LOW)
        right, send = lax.optimization_barrier((right, send))
        total = self.outer.scatter(product_left(left[:, :half], right), send)
        padded = self.weights.padded
        keep = total[:padded]
        got = self.partner(total[padded:].astype(LOW)).astype(jnp.float32)
        first = jnp.where(self.core == 0, keep, got)[: self.rows]
        second = jnp.where(self.core == 0, got, keep)[: self.rows]
        shape = (self.rows, 2, -1, self.run)
        block = jnp.stack([first.reshape(shape), second.reshape(shape)], axis=3)
        return right, (block[:, 0].reshape(-1), block[:, 1].reshape(-1))


class FlatFeed:
    def __init__(self):
        self.weights = FlatWeights()

    def gather(self, gate, up, down):
        return self.weights.gather((gate, up), (FF, FF)), self.weights.gather((down,), (D,))

    def both(self, values):
        return values

    def own(self, values):
        return values

    def scatter_down(self, active, cotangent):
        cotangent, (grad,) = self.weights.scatter(active, cotangent, (D,))
        return cotangent, grad

    def scatter(self, left, right):
        return self.weights.scatter(left, right, (FF, FF))


class FlatWeights:
    def gather(self, flats, widths):
        return jnp.concatenate(
            [
                lax.all_gather(flat, BOTH, axis=0, tiled=True).reshape(-1, width)
                for flat, width in zip(flats, widths)
            ],
            axis=1,
        )

    def spread(self, values):
        return values.astype(LOW)

    def unspread(self, values):
        return values

    def scatter(self, left, right, widths):
        cuts = [sum(widths[:index]) for index in range(len(widths) + 1)]
        return right, [
            lax.psum_scatter(
                product_left(left, right[:, low:high]).astype(LOW).reshape(-1),
                BOTH,
                scatter_dimension=0,
                tiled=True,
            ).astype(jnp.float32)
            for low, high in zip(cuts[:-1], cuts[1:])
        ]


def rope_tables(places):
    half = HEAD_DIM // 2
    frequency = THETA ** (-jnp.arange(half, dtype=jnp.float32) * 2.0 / HEAD_DIM)
    angle = places.astype(jnp.float32)[:, None] * frequency[None, :]
    return (jnp.cos(angle)[:, None, :], jnp.sin(angle)[:, None, :])


def rotate(values, cosine, sine, direction):
    half = HEAD_DIM // 2
    shaped = values.reshape(values.shape[0], -1, HEAD_DIM)
    first = shaped[..., :half]
    second = shaped[..., half:]
    turned = jnp.concatenate(
        [first * cosine - direction * second * sine, second * cosine + direction * first * sine],
        axis=-1,
    )
    return turned.reshape(values.shape)


def rms_forward(values, gain):
    factor = lax.rsqrt(jnp.mean(values * values, axis=-1, keepdims=True) + EPSILON)
    return (values * factor * gain, factor)


def rms_backward(values, factor, gain, grad):
    inner = grad * gain
    gain_grad = jnp.sum(grad * values * factor, axis=0)
    cube = factor * factor * factor
    input_grad = factor * inner - values * cube * jnp.mean(inner * values, axis=-1, keepdims=True)
    return (input_grad, gain_grad)


def per_device(
    dp_size,
    ctx_size,
    tokens,
    w_query,
    w_key,
    w_value,
    w_out,
    w_gate,
    w_up,
    w_down,
    norm_gains,
    cotangent,
):
    local_rows = tokens.shape[0]
    query_width = HEADS * HEAD_DIM
    pair_width = KV_HEADS * HEAD_DIM
    groups = HEADS // KV_HEADS
    scale = HEAD_DIM ** (-0.5)
    devices = dp_size * ctx_size
    by_rows = D % devices == 0 and FF % devices == 0

    qkv_widths = (query_width, pair_width, pair_width)
    if by_rows:
        dp_bits = bits_of(dp_size)[1:]
        rows = D // devices
        stages = [("ctx", mask) for mask in reversed(bits_of(ctx_size))]
        stages += [("dp", mask) for mask in dp_bits] + [("dp", 1)]
        attn = RowWeights(Exchange(dp_size, ctx_size, stages), rows)
        feed = SplitFeed(dp_size, ctx_size, rows, FF // devices, dp_bits[::-1], dp_bits)
    else:
        attn, feed = FlatWeights(), FlatFeed()

    gains = lax.all_gather(norm_gains, "dp", axis=1, tiled=True).astype(jnp.float32)
    qkv_matrix = attn.gather((w_query, w_key, w_value), qkv_widths)
    out_matrix = attn.gather((w_out,), (D,))
    feed_matrix, down_matrix = feed.gather(w_gate, w_up, w_down)
    all_cotangents = feed.both(cotangent)

    ctx_place = lax.axis_index("ctx")
    inner = jnp.arange(local_rows, dtype=jnp.int32)
    places = ctx_place * local_rows + inner
    others = ctx_place ^ jnp.arange(ctx_size, dtype=jnp.int32)
    key_places = (others[:, None] * local_rows + inner[None, :]).reshape(-1)
    cosine, sine = rope_tables(places)

    inputs = tokens.astype(jnp.float32)
    scaled_first, rms_first = rms_forward(inputs, gains[0])
    normed_first = attn.spread(scaled_first.astype(LOW))
    projected = product(normed_first, qkv_matrix)
    query = rotate(projected[:, :query_width], cosine, sine, 1.0).astype(LOW)
    key = rotate(projected[:, query_width : query_width + pair_width], cosine, sine, 1.0)
    pairs = jnp.concatenate([key.astype(LOW), projected[:, query_width + pair_width :].astype(LOW)], 1)
    whole = jnp.concatenate(
        [pairs] + [swap(pairs, "ctx", ctx_size, mask) for mask in range(1, ctx_size)], axis=0
    )
    count = whole.shape[0]

    def by_head(values):
        shaped = values.reshape(local_rows, KV_HEADS, groups, HEAD_DIM).transpose(1, 2, 0, 3)
        return shaped.reshape(KV_HEADS, groups * local_rows, HEAD_DIM)

    def by_token(values):
        shaped = values.reshape(KV_HEADS, groups, local_rows, HEAD_DIM).transpose(2, 0, 1, 3)
        return shaped.reshape(local_rows, query_width)

    def batched(pattern, left, right):
        return jnp.einsum(pattern, left, right, preferred_element_type=jnp.float32)

    query_heads = by_head(query)
    key_heads = whole[:, :pair_width].reshape(count, KV_HEADS, HEAD_DIM).transpose(1, 0, 2)
    value_heads = whole[:, pair_width:].reshape(count, KV_HEADS, HEAD_DIM).transpose(1, 0, 2)
    allowed = jnp.tile(places, groups)[:, None] >= key_places[None, :]
    scores = batched("gqd,gkd->gqk", query_heads, key_heads) * scale
    scores = jnp.where(allowed[None], scores, -1e30)
    top = jnp.max(scores, axis=-1, keepdims=True)
    unscaled = jnp.exp(scores - top)
    weights = unscaled * (1.0 / jnp.sum(unscaled, axis=-1, keepdims=True))
    weights_low = weights.astype(LOW)
    mixed_heads = batched("gqk,gkd->gqd", weights_low, value_heads)
    mixed_low = attn.spread(by_token(mixed_heads.astype(LOW)))

    hidden = inputs + product(mixed_low, out_matrix)
    scaled_second, rms_second = rms_forward(hidden, gains[1])
    normed_second = feed.weights.spread(feed.both(scaled_second.astype(LOW)))
    gate_up = product(normed_second, feed_matrix)
    units = gate_up.shape[1] // 2
    gate_values, up_values = gate_up[:, :units], gate_up[:, units:]
    sigmoid_gate = jax.nn.sigmoid(gate_values)
    silu_gate = gate_values * sigmoid_gate
    active = (silu_gate * up_values).astype(LOW)
    layer_out = (hidden + feed.own(product(active, down_matrix))).astype(LOW)

    all_cotangents, grad_down = feed.scatter_down(active, all_cotangents)
    grad_layer = cotangent.astype(jnp.float32)
    grad_active = product_right(all_cotangents, down_matrix)
    grad_gate_values = grad_active * up_values * (
        sigmoid_gate * (1.0 + gate_values * (1.0 - sigmoid_gate))
    )
    grad_feed = jnp.concatenate(
        [grad_gate_values.astype(LOW), (grad_active * silu_gate).astype(LOW)], axis=1
    )
    grad_feed, (grad_gate, grad_up) = feed.scatter(normed_second, grad_feed)
    grad_normed_second = feed.own(feed.weights.unspread(product_right(grad_feed, feed_matrix)))
    grad_hidden_norm, gain_second = rms_backward(hidden, rms_second, gains[1], grad_normed_second)
    grad_hidden = grad_layer + grad_hidden_norm
    grad_attn = grad_hidden.astype(LOW)
    grad_attn, (grad_out,) = attn.scatter(mixed_low, grad_attn, (D,))
    grad_mixed = attn.unspread(product_right(grad_attn, out_matrix)).astype(LOW)

    grad_heads = by_head(grad_mixed)
    delta = jnp.sum(grad_heads.astype(jnp.float32) * mixed_heads, axis=-1, keepdims=True)
    grad_weights = batched("gqd,gkd->gqk", grad_heads, value_heads)
    grad_scores = (weights * (grad_weights - delta)).astype(LOW)
    grad_key_all = batched("gqk,gqd->gkd", grad_scores, query_heads) * scale
    grad_value_all = batched("gqk,gqd->gkd", weights_low, grad_heads)
    grad_query_heads = batched("gqk,gkd->gqd", grad_scores, key_heads) * scale
    term = jnp.concatenate([grad_key_all, grad_value_all], axis=0)
    term = term.transpose(1, 0, 2).reshape(ctx_size, local_rows, 2 * pair_width)
    pair_grads = term[0]
    for mask in range(1, ctx_size):
        pair_grads += swap(term[mask].astype(LOW), "ctx", ctx_size, mask).astype(jnp.float32)
    grad_projected = jnp.concatenate(
        [
            rotate(by_token(grad_query_heads), cosine, sine, -1.0).astype(LOW),
            rotate(pair_grads[:, :pair_width], cosine, sine, -1.0).astype(LOW),
            pair_grads[:, pair_width:].astype(LOW),
        ],
        axis=1,
    )
    grad_projected, (grad_query, grad_key, grad_value) = attn.scatter(
        normed_first, grad_projected, qkv_widths
    )
    grad_normed_first = attn.unspread(product_right(grad_projected, qkv_matrix))
    grad_input_norm, gain_first = rms_backward(inputs, rms_first, gains[0], grad_normed_first)
    grad_tokens = (grad_hidden + grad_input_norm).astype(LOW)
    gain_total = sum_gains(jnp.stack([gain_first, gain_second]), dp_size, ctx_size)
    return (
        layer_out,
        grad_tokens,
        grad_query,
        grad_key,
        grad_value,
        grad_out,
        grad_gate,
        grad_up,
        grad_down,
        gain_total,
    )


def solution(mesh):
    placed = (
        P(("dp", "ctx"), None),
        P(("dp", "ctx")),
        P(("dp", "ctx")),
        P(("dp", "ctx")),
        P(("dp", "ctx")),
        P(("dp", "ctx")),
        P(("dp", "ctx")),
        P(("dp", "ctx")),
        P(None, "dp"),
        P(("dp", "ctx"), None),
    )
    dp_size, ctx_size = mesh.shape["dp"], mesh.shape["ctx"]
    return jax.shard_map(
        functools.partial(per_device, dp_size, ctx_size),
        mesh=mesh,
        in_specs=placed,
        out_specs=(
            P(("dp", "ctx"), None),
            P(("dp", "ctx"), None),
            P(("dp", "ctx")),
            P(("dp", "ctx")),
            P(("dp", "ctx")),
            P(("dp", "ctx")),
            P(("dp", "ctx")),
            P(("dp", "ctx")),
            P(("dp", "ctx")),
            P(None, "dp"),
        ),
        check_vma=False,
    )
```
